32 devices in a mesh: groups: 2 (over y), tensor: 4 (over z), section: 2 (over x), pool: 2 (over core).
Axes of the slice: x: 2, y: 2, z: 4, core: 2. Of those that a mesh axis runs over, the one named last changes fastest.
Arguments:
- cotangent: bfloat16 [6, 256, 8192], P('groups', None, ('tensor', 'pool')), parts along dimension 0, may hold values from -6 to 6
- saved_inputs: bfloat16 [2, 6, 256, 8192], P('section', 'groups', None, ('tensor', 'pool')), parts along dimension 1, may hold values from -6 to 6
- base_weight: bfloat16 [2, 8192, 4, 2, 1024], P('section', 'tensor', None, 'pool'), may hold values from -0.0625 to 0.0625
- panel_a: bfloat16 [2, 16, 64, 8192], P('section', 'pool', None, 'tensor'), may hold values from -0.0625 to 0.0625
- panel_b: bfloat16 [2, 16, 64, 8192], P('section', 'pool', None, 'tensor'), may hold values from -0.75 to 0.75
- seg_tiles: int32 [8], P('groups'), parts along dimension 0, may hold values from 1 to 2, 6 in all
- seg_adapter: int32 [8], P('groups'), parts along dimension 0, may hold values from 0 to 15
- slot_of: int32 [16], replicated, may hold values from 0 to 15, each once
Outputs:
- grad_inputs: bfloat16 [2, 6, 256, 8192], P('section', 'groups', None, ('tensor', 'pool')), parts along dimension 1
- grad_a: float32 [2, 32, 64, 8192], P('section', 'groups', None, ('tensor', 'pool')), parts along dimension 1
- grad_b: float32 [2, 32, 64, 8192], P('section', 'groups', None, ('tensor', 'pool')), parts along dimension 1
The draws below stay inside these ranges and needn't reach their ends.
There are 2 independent parts, one for each index of `groups`. The reference program is written for one: setup_inputs(seed, part) draws one part's arguments, and reference() takes and returns one part's arrays. A program takes and returns all parts, laid end to end along the dimension named above; an argument that names none is the same for every part. Nothing has to cross between parts.
Inputs may be any that keep to these rules, and one draw needn't show every extreme that they name: `seg_tiles`: two segments cover 2 tiles each, all others 1, and the segments cover all 6 tiles. `slot_of`: each slot holds one adapter.
All inputs are finite; a program needn't handle non-finite values.
Results may differ from the reference program's by a relative error of at most 0.0048.
Values may be sent and summed in bfloat16 or wider, within the bound.
A program may use at most 192 MiB of HBM per device.

```python
import math
import jax
import jax.numpy as jnp
import numpy as np
from jax import lax

MODEL_WIDTH = 8192
RANK = 64
ADAPTERS = 16
MICRO = 3
ROWS = 256
TILE = 128
SECTIONS = 2
TILES = 6
SEGS = 4
N_TENSOR = 4
N_POOL = 2


def set_ends(drawn, stream_key, low, top_value):
    longest = drawn.shape.index(max(drawn.shape))
    spots = []
    for shift in (0, 1):
        where = [jax.random.randint(jax.random.fold_in(stream_key, axis), (), 0, length) for axis, length in enumerate(drawn.shape)]
        where[longest] = (where[longest] + shift) % drawn.shape[longest]
        spots.append(tuple(where))
    return drawn.at[spots[0]].set(low).at[spots[1]].set(top_value)


def block_scale(stream_key, dims, pieces, low, top_value):
    level = 1.0
    for position, shards_of in pieces:
        draws = jax.random.uniform(jax.random.fold_in(jax.random.fold_in(stream_key, 6), position), (shards_of,), jnp.float32, low / len(pieces), top_value / len(pieces))
        level = level * jnp.repeat(jnp.exp(draws), dims[position] // shards_of).reshape((-1,) + (1,) * (len(dims) - 1 - position))
    return level


def split_up(count, total, limit, skew):
    portions = [(1 << 20) // math.isqrt(grade ** skew) + 1 for grade in range(2, count + 1)]
    spare, counts = total - limit - (count - 1), [1] * (count - 1)
    while spare > 0:
        free = [i for i in range(count - 1) if counts[i] < limit]
        whole, budget = sum([portions[i] for i in free]), spare
        for i in free:
            addition = min(limit - counts[i], max(1, budget * portions[i] // whole), spare)
            counts[i] = counts[i] + addition
            spare = spare - addition
    return np.array([limit] + counts)


def uneven_parts(stream_key, number_of, total, reach, skew):
    if number_of == 2:
        one = jax.random.randint(stream_key, (), max(1, total - reach), min(reach, total - 1) + 1)
        return jnp.stack([one, total - one])
    lengths = jnp.asarray(split_up(number_of, total, reach, skew), jnp.int32)
    pairs = (number_of - 1) // 2
    giver, sink = lengths[1:1 + 2 * pairs:2], lengths[2:2 + 2 * pairs:2]
    room = jnp.minimum(giver - 1, reach - sink)
    shifted = jax.random.randint(jax.random.fold_in(stream_key, 1), (pairs,), 0, 1 << 20) % (room + 1)
    lengths = lengths.at[1:1 + 2 * pairs:2].set(giver - shifted).at[2:2 + 2 * pairs:2].set(sink + shifted)
    return lengths[jax.random.permutation(jax.random.fold_in(stream_key, 2), number_of)]


def gaussian(own_key, shape, scale, reach, cuts=(), held_as=jnp.bfloat16):
    values = scale * jax.random.normal(own_key, shape, jnp.float32)
    if cuts:
        values = values * block_scale(own_key, shape, cuts, -0.22, 0.18)
    return jnp.clip(values, -reach, reach).astype(held_as)


def setup_inputs(seed: int = 0, part: int = 0) -> dict:
    key_list = jax.random.split(jax.random.key(seed), 9)
    part_splits = jax.random.split(jax.random.fold_in(key_list[8], part), 9)
    return {
        "cotangent": gaussian(part_splits[0], (MICRO, ROWS, MODEL_WIDTH), 1.0, 6.0, ((2, 8),)),
        "saved_inputs": gaussian(part_splits[1], (SECTIONS, MICRO, ROWS, MODEL_WIDTH), 1.0, 6.0, ((0, 2), (3, 8))),
        "base_weight": gaussian(key_list[2], (SECTIONS, MODEL_WIDTH, N_TENSOR, N_POOL, MODEL_WIDTH // (N_TENSOR * N_POOL)), MODEL_WIDTH ** -0.5, 0.0625, ((0, 2), (1, 4), (3, 2))),
        "panel_a": gaussian(key_list[3], (SECTIONS, ADAPTERS, RANK, MODEL_WIDTH), MODEL_WIDTH ** -0.5, 0.0625, ((0, 2), (1, 2), (3, 4))),
        "panel_b": gaussian(key_list[4], (SECTIONS, ADAPTERS, RANK, MODEL_WIDTH), RANK ** -0.5, 0.75, ((0, 2), (1, 2), (3, 4))),
        "seg_tiles": uneven_parts(part_splits[5], SEGS, TILES, 2, 0).astype(jnp.int32),
        "seg_adapter": set_ends(jax.random.randint(part_splits[6], (SEGS,), 0, ADAPTERS), jax.random.fold_in(part_splits[6], 1), 0, ADAPTERS - 1).astype(jnp.int32),
        "slot_of": jax.random.permutation(key_list[7], ADAPTERS).astype(jnp.int32),
    }


adapter_scale = 0.5


def tile_owners(seg_tiles, seg_adapter):
    ends = jnp.cumsum(seg_tiles).astype(jnp.int32)
    places = jnp.arange(TILES, dtype=jnp.int32)
    segment = jnp.sum((ends[None, :] <= places[:, None]).astype(jnp.int32), axis=1)
    picks = segment[:, None] == jnp.arange(SEGS, dtype=jnp.int32)[None, :]
    return jnp.sum(jnp.where(picks, seg_adapter[None, :], 0), axis=1).astype(jnp.int32)


def reference(cotangent, saved_inputs, base_weight, panel_a, panel_b, seg_tiles, seg_adapter, slot_of):
    tile_adapter = tile_owners(seg_tiles, seg_adapter)
    tile_slot = slot_of[tile_adapter]
    weights = base_weight.reshape(SECTIONS, MODEL_WIDTH, MODEL_WIDTH)
    grads = cotangent
    list_in, list_a, list_b = [], [], []
    for section in range(SECTIONS - 1, -1, -1):
        panels_a = panel_a[section][tile_slot].astype(jnp.float32)
        panels_b = panel_b[section][tile_slot].astype(jnp.float32)
        input_cube3 = saved_inputs[section].reshape(TILES, TILE, MODEL_WIDTH).astype(jnp.float32)
        gradient_cube3 = grads.reshape(TILES, TILE, MODEL_WIDTH).astype(jnp.float32)
        shrink_in = jnp.einsum("tkd,trd->tkr", input_cube3, panels_a, precision=lax.Precision.HIGHEST)
        shrink_out = jnp.einsum("tkd,trd->tkr", gradient_cube3, panels_b, precision=lax.Precision.HIGHEST)
        lowrank_input = lax.optimization_barrier(shrink_in.astype(jnp.bfloat16)).astype(jnp.float32)
        lowrank_output = lax.optimization_barrier(shrink_out.astype(jnp.bfloat16)).astype(jnp.float32)
        base_matrix = jnp.dot(grads.reshape(-1, MODEL_WIDTH), weights[section].T, preferred_element_type=jnp.float32)
        expand_rows = jnp.einsum("tkr,trd->tkd", lowrank_output, panels_a, precision=lax.Precision.HIGHEST)
        backward_result = (base_matrix + adapter_scale * expand_rows.reshape(-1, MODEL_WIDTH)).astype(jnp.bfloat16)
        update_first = adapter_scale * jnp.einsum("fcj,fcm->fjm", lowrank_output, input_cube3, precision=lax.Precision.HIGHEST)
        update_second = adapter_scale * jnp.einsum("fcj,fcm->fjm", lowrank_input, gradient_cube3, precision=lax.Precision.HIGHEST)
        grad_a = jnp.zeros((ADAPTERS, RANK, MODEL_WIDTH), jnp.float32).at[tile_adapter].add(update_first)
        grad_b = jnp.zeros((ADAPTERS, RANK, MODEL_WIDTH), jnp.float32).at[tile_adapter].add(update_second)
        grads = backward_result.reshape(MICRO, ROWS, MODEL_WIDTH)
        list_in.append(grads)
        list_a.append(grad_a)
        list_b.append(grad_b)
    return (jnp.stack(list_in[::-1]), jnp.stack(list_a[::-1]), jnp.stack(list_b[::-1]))
```

```python
import jax
import jax.numpy as jnp
from jax import lax
from jax.experimental import pallas as pl
from jax.experimental.pallas import tpu as pltpu
from jax.sharding import PartitionSpec as P

TILE = 128
SCALE = 0.5
AHEAD = 2
MESH = pl.DeviceIdType.MESH
F32 = jnp.float32
BF16 = jnp.bfloat16


def tile_owners(seg_tiles, seg_adapter, tiles):
    segs = seg_tiles.shape[0]
    ends = jnp.cumsum(seg_tiles)
    places = jnp.arange(tiles, dtype=jnp.int32)
    segment = jnp.sum((ends[None, :] <= places[:, None]).astype(jnp.int32), axis=1)
    picks = segment[:, None] == jnp.arange(segs, dtype=jnp.int32)[None, :]
    return jnp.sum(jnp.where(picks, seg_adapter[None, :], 0), axis=1)


def row_dot(a, b):
    return lax.dot_general(a, b, (((1,), (1,)), ((), ())), preferred_element_type=F32)


def kernel(
    seg_tiles, seg_adapter, slot_of, cot, x, w_hbm, panel_a, panel_b,
    grad_in, grad_own, low_u, low_h,
    w, gath, part, part_in, own_acc, sel_a, sel_b, put_a, put_b,
    u_part, u_pool, u_sum, u_all, h_part, h_pool, h_sum, h_all,
    w_sem, g_send, g_recv, u_send, u_recv, up_send, up_recv, pp_send, pp_recv,
    sel_send, sel_recv, hp_send, hp_recv, h_send, h_recv, s_send, s_recv,
):
    n = lax.axis_size("tensor")
    top = lax.axis_size("section") - 1
    s, t, p = lax.axis_index("section"), lax.axis_index("tensor"), lax.axis_index("pool")
    q = 1 - p
    rows_all, width = cot.shape
    tiles = rows_all // TILE
    segs = seg_tiles.shape[0]
    slots = panel_a.shape[0]
    block = min(256, width)

    barrier = pltpu.get_barrier_semaphore()

    def greet(i, _):
        pl.semaphore_signal(barrier, inc=1, device_id={"tensor": lax.rem(t + i, n)}, device_id_type=MESH)
        return 0

    lax.fori_loop(1, n, greet, 0)
    pl.semaphore_signal(barrier, inc=1, device_id={"pool": q}, device_id_type=MESH)

    @pl.when(s > 0)
    def _():
        pl.semaphore_signal(barrier, inc=1, device_id={"section": s - 1}, device_id_type=MESH)

    @pl.when(s < top)
    def _():
        pl.semaphore_signal(barrier, inc=1, device_id={"section": s + 1}, device_id_type=MESH)

    w_copy = pltpu.make_async_copy(w_hbm, w, w_sem)
    w_copy.start()
    pl.semaphore_wait(barrier, n + (s > 0).astype(jnp.int32) + (s < top).astype(jnp.int32))

    def rows(k):
        return pl.ds(pl.multiple_of(k * TILE, TILE), TILE)

    def gather_copy(k, sender, target):
        place = gath.at[sender, rows(k)]
        return pltpu.make_async_remote_copy(
            place, place, g_send.at[k, target], g_recv.at[k, sender],
            device_id={"tensor": target}, device_id_type=MESH)

    def u_copy(k, sender, target):
        return pltpu.make_async_remote_copy(
            u_sum.at[k], u_all.at[k, sender], u_send.at[k, target], u_recv.at[k, sender],
            device_id={"tensor": target}, device_id_type=MESH)

    def h_copy(sender, target):
        return pltpu.make_async_remote_copy(
            h_sum, h_all.at[sender], h_send.at[target], h_recv.at[sender],
            device_id={"tensor": target}, device_id_type=MESH)

    def pool_copy(source, dest, send, recv):
        return pltpu.make_async_remote_copy(
            source, dest, send, recv, device_id={"pool": q}, device_id_type=MESH)

    def section_copy(k):
        return pltpu.make_async_remote_copy(
            grad_in.at[rows(k)], gath.at[t, rows(k)], s_send.at[k], s_recv.at[k],
            device_id={"section": jnp.maximum(s - 1, 0)}, device_id_type=MESH)

    def others(body):
        def run(i, _):
            body(lax.rem(t + i, n))
            return 0

        lax.fori_loop(1, n, run, 0)

    @pl.when(s == top)
    def _():
        gath[t] = cot[...]

        def first(k, _):
            others(lambda tt: gather_copy(k, t, tt).start())
            return 0

        lax.fori_loop(0, min(AHEAD, tiles), first, 0)

    mine = pl.ds(pl.multiple_of(p * width, width), width)
    theirs = pl.ds(pl.multiple_of(q * width, width), width)
    seg_slot = [slot_of[seg_adapter[j]] for j in range(segs)]
    for j in range(segs):
        local = jnp.clip(seg_slot[j] - p * slots, 0, slots - 1)
        put_b[j] = panel_b[local, :, theirs]
        sel_b[0, j] = panel_b[local, :, mine]
    copy_b = pool_copy(put_b, sel_b.at[1], sel_send.at[0], sel_recv.at[0])
    copy_b.start()
    for j in range(segs):
        local = jnp.clip(seg_slot[j] - p * slots, 0, slots - 1)
        put_a[j] = panel_a[local, :, theirs]
        sel_a[0, j] = panel_a[local, :, mine]
    copy_a = pool_copy(put_a, sel_a.at[1], sel_send.at[1], sel_recv.at[1])
    copy_a.start()
    copy_b.wait()
    copy_a.wait()

    def chosen(k, sel):
        total, segment = jnp.int32(0), jnp.int32(0)
        for j in range(segs - 1):
            total = total + seg_tiles[j]
            segment = segment + (total <= k).astype(jnp.int32)
        slot = slot_of[seg_adapter[segment]]
        home = (slot >= p * slots) & (slot < (p + 1) * slots)
        return sel[1 - home.astype(jnp.int32), segment]

    def launch(k):
        @pl.when(s < top)
        def _():
            section_copy(k).wait_recv()
            others(lambda tt: gather_copy(k, t, tt).start())

        u_part[k] = row_dot(chosen(k, sel_b), gath[t, rows(k)])
        pool_copy(u_part.at[k], u_pool.at[k], up_send.at[k], up_recv.at[k]).start()

    launch(0)

    def shrink_x(k, _):
        h_part[:, rows(k)] = row_dot(chosen(k, sel_a), x[rows(k)])
        return 0

    lax.fori_loop(0, tiles, shrink_x, 0)
    h_pool_copy = pool_copy(h_part, h_pool, hp_send, hp_recv)
    h_pool_copy.start()
    w_copy.wait()
    h_pool_copy.wait()
    h_sum[...] = h_part[...] + h_pool[...]
    others(lambda tt: h_copy(t, tt).start())

    def multiply(k, tt, half, acc, fresh):
        def one(b, _):
            r = pl.multiple_of(b * block, block)
            wr = pl.ds(pl.multiple_of(half * width + r, block), block)
            wc = pl.ds(pl.multiple_of(tt * width, width), width)
            product = row_dot(gath[tt, rows(k)], w[wr, wc])
            if fresh:
                acc[:, pl.ds(r, block)] = product
            else:
                acc[:, pl.ds(r, block)] += product
            return 0

        lax.fori_loop(0, width // block, one, 0)

    def process(k, _):
        @pl.when(k + 1 < tiles)
        def _():
            launch(k + 1)

        pool_copy(u_part.at[k], u_pool.at[k], up_send.at[k], up_recv.at[k]).wait()
        u_sum[k] = u_part[k] + u_pool[k]
        others(lambda tt: u_copy(k, t, tt).start())

        send = part.at[k]
        multiply(k, t, q, send, True)
        multiply(k, t, p, own_acc, True)

        def middle(i, _):
            tt = lax.rem(t + i, n)
            gather_copy(k, tt, tt).wait_recv()
            multiply(k, tt, q, send, False)
            multiply(k, tt, p, own_acc, False)
            return 0

        lax.fori_loop(1, n - 1, middle, 0)
        last = lax.rem(t + n - 1, n)
        gather_copy(k, last, last).wait_recv()

        @pl.when((s == top) & (k + AHEAD < tiles))
        def _():
            others(lambda tt: gather_copy(k + AHEAD, t, tt).start())

        multiply(k, last, q, send, False)
        half_copy = pool_copy(send, part_in.at[k], pp_send.at[k], pp_recv.at[k])
        half_copy.start()
        multiply(k, last, p, own_acc, False)
        u_all[k, t] = u_sum[k]
        others(lambda tt: u_copy(k, tt, tt).wait_recv())
        u = u_all[k, 0]
        for i in range(1, n):
            u = u + u_all[k, i]
        low_u[:, rows(k)] = u.astype(BF16)
        expand = jnp.dot(u.T.astype(BF16), chosen(k, sel_a), preferred_element_type=F32)
        half_copy.wait()
        grad_in[rows(k)] = (own_acc[...] + part_in[k] + SCALE * expand).astype(BF16)

        @pl.when(s > 0)
        def _():
            section_copy(k).start()

        return 0

    lax.fori_loop(0, tiles, process, 0)

    grad_own[...] = gath[t]
    h_all[t] = h_sum[...]
    others(lambda tt: h_copy(tt, tt).wait_recv())
    h = h_all[0]
    for i in range(1, n):
        h = h + h_all[i]
    low_h[...] = h.astype(BF16)

    def sent(tt):
        h_copy(t, tt).wait_send()

        def one(k, _):
            gather_copy(k, t, tt).wait_send()
            u_copy(k, t, tt).wait_send()
            return 0

        lax.fori_loop(0, tiles, one, 0)

    others(sent)

    @pl.when(s > 0)
    def _():
        def one(k, _):
            section_copy(k).wait_send()
            return 0

        lax.fori_loop(0, tiles, one, 0)


def per_device(cotangent, saved_inputs, base_weight, panel_a, panel_b, seg_tiles, seg_adapter, slot_of):
    n = lax.axis_size("tensor")
    micro, row_count, width = cotangent.shape
    m = micro * row_count
    tiles = m // TILE
    weight = base_weight[0].reshape(base_weight.shape[1], -1)
    x = saved_inputs[0].reshape(m, width)
    rank = panel_a.shape[2]
    segs = seg_tiles.shape[0]
    smem = pl.BlockSpec(memory_space=pltpu.SMEM)
    vmem = pl.BlockSpec(memory_space=pltpu.VMEM)
    dma = pltpu.SemaphoreType.DMA
    grad_in, grad_own, low_u, low_h = pl.pallas_call(
        kernel,
        out_shape=(
            jax.ShapeDtypeStruct((m, width), BF16),
            jax.ShapeDtypeStruct((m, width), BF16),
            jax.ShapeDtypeStruct((rank, m), BF16),
            jax.ShapeDtypeStruct((rank, m), BF16),
        ),
        in_specs=[smem] * 3 + [vmem] * 2 + [pl.BlockSpec(memory_space=pl.ANY)] + [vmem] * 2,
        out_specs=(vmem,) * 4,
        scratch_shapes=[
            pltpu.VMEM(weight.shape, BF16),
            pltpu.VMEM((n, m, width), BF16),
            pltpu.VMEM((tiles, TILE, width), F32),
            pltpu.VMEM((tiles, TILE, width), F32),
            pltpu.VMEM((TILE, width), F32),
            pltpu.VMEM((2, segs, rank, width), BF16),
            pltpu.VMEM((2, segs, rank, width), BF16),
            pltpu.VMEM((segs, rank, width), BF16),
            pltpu.VMEM((segs, rank, width), BF16),
            pltpu.VMEM((tiles, rank, TILE), F32),
            pltpu.VMEM((tiles, rank, TILE), F32),
            pltpu.VMEM((tiles, rank, TILE), F32),
            pltpu.VMEM((tiles, n, rank, TILE), F32),
            pltpu.VMEM((rank, m), F32),
            pltpu.VMEM((rank, m), F32),
            pltpu.VMEM((rank, m), F32),
            pltpu.VMEM((n, rank, m), F32),
            dma(()),
            dma((tiles, n)), dma((tiles, n)), dma((tiles, n)), dma((tiles, n)),
            dma((tiles,)), dma((tiles,)), dma((tiles,)), dma((tiles,)),
            dma((2,)), dma((2,)), dma(()), dma(()), dma((n,)), dma((n,)),
            dma((tiles,)), dma((tiles,)),
        ],
        compiler_params=pltpu.CompilerParams(
            collective_id=0, has_side_effects=True, vmem_limit_bytes=58 * 1024 * 1024),
    )(seg_tiles, seg_adapter, slot_of, cotangent.reshape(m, width), x, weight, panel_a[0], panel_b[0])

    adapters = slot_of.shape[0]
    owners = jnp.repeat(tile_owners(seg_tiles, seg_adapter, tiles), TILE)
    hit = owners[None, :] == jnp.arange(adapters, dtype=jnp.int32)[:, None]

    def spread(low, wide):
        lanes = jnp.where(hit[:, None, :], low[None], jnp.zeros((), BF16)).reshape(adapters * rank, m)
        full = SCALE * jnp.dot(lanes, wide, preferred_element_type=F32)
        return full.reshape(1, adapters, rank, width)

    return (grad_in.reshape(1, micro, row_count, width), spread(low_u, x), spread(low_h, grad_own))


def solution(mesh):
    placed = (
        P("groups", None, ("tensor", "pool")),
        P("section", "groups", None, ("tensor", "pool")),
        P("section", "tensor", None, "pool", None),
        P("section", "pool", None, "tensor"),
        P("section", "pool", None, "tensor"),
        P("groups"),
        P("groups"),
        P(),
    )
    out = P("section", "groups", None, ("tensor", "pool"))
    return jax.shard_map(
        per_device, mesh=mesh, in_specs=placed, out_specs=(out, out, out), check_vma=False)
```

```python
import jax
import jax.numpy as jnp
from jax import lax
from jax.experimental import pallas as pl
from jax.experimental.pallas import tpu as pltpu
from jax.sharding import PartitionSpec as P

TILE = 128
SCALE = 0.5
AHEAD = 2
MESH = pl.DeviceIdType.MESH
F32 = jnp.float32
BF16 = jnp.bfloat16


def tile_owners(seg_tiles, seg_adapter, tiles):
    segs = seg_tiles.shape[0]
    ends = jnp.cumsum(seg_tiles)
    places = jnp.arange(tiles, dtype=jnp.int32)
    segment = jnp.sum((ends[None, :] <= places[:, None]).astype(jnp.int32), axis=1)
    picks = segment[:, None] == jnp.arange(segs, dtype=jnp.int32)[None, :]
    return jnp.sum(jnp.where(picks, seg_adapter[None, :], 0), axis=1)


def row_dot(a, b):
    return lax.dot_general(a, b, (((1,), (1,)), ((), ())), preferred_element_type=F32)


def kernel(
    seg_tiles, seg_adapter, slot_of, cot, x, w_hbm, panel_a, panel_b,
    grad_in, grad_own, low_u, low_h,
    w, gath, part, part_in, own_acc, sel_a, sel_b, put_a, put_b,
    u_part, u_pool, u_sum, u_all, h_part, h_pool, h_sum, h_all,
    w_sem, g_send, g_down, g_recv, u_send, u_recv, up_send, up_recv, pp_send, pp_recv,
    sel_send, sel_recv, hp_send, hp_recv, h_send, h_recv, s_send, s_recv,
):
    n = lax.axis_size("tensor")
    top = lax.axis_size("section") - 1
    s, t, p = lax.axis_index("section"), lax.axis_index("tensor"), lax.axis_index("pool")
    q = 1 - p
    rows_all, width = cot.shape
    tiles = rows_all // TILE
    segs = seg_tiles.shape[0]
    slots = panel_a.shape[0]
    block = min(256, width)

    barrier = pltpu.get_barrier_semaphore()

    def greet(i, _):
        pl.semaphore_signal(barrier, inc=1, device_id={"tensor": lax.rem(t + i, n)}, device_id_type=MESH)
        return 0

    lax.fori_loop(1, n, greet, 0)
    pl.semaphore_signal(barrier, inc=1, device_id={"pool": q}, device_id_type=MESH)

    @pl.when(s > 0)
    def _():
        pl.semaphore_signal(barrier, inc=1, device_id={"section": s - 1}, device_id_type=MESH)

    @pl.when(s < top)
    def _():
        pl.semaphore_signal(barrier, inc=1, device_id={"section": s + 1}, device_id_type=MESH)

    w_copy = pltpu.make_async_copy(w_hbm, w, w_sem)
    w_copy.start()
    pl.semaphore_wait(barrier, n + (s > 0).astype(jnp.int32) + (s < top).astype(jnp.int32))

    def rows(k):
        return pl.ds(pl.multiple_of(k * TILE, TILE), TILE)

    def block_copy(k, owner, target, sem):
        place = gath.at[owner, rows(k)]
        return pltpu.make_async_remote_copy(
            place, place, sem, g_recv.at[k, owner],
            device_id={"tensor": target}, device_id_type=MESH)

    def upward(k, owner):
        return block_copy(k, owner, jnp.minimum(t + 1, n - 1), g_send.at[k, owner])

    def downward(k, owner):
        sem = g_send.at[k, owner] if owner is not t else g_down.at[k]
        return block_copy(k, owner, jnp.maximum(t - 1, 0), sem)

    def own_start(k):
        @pl.when(t < n - 1)
        def _():
            upward(k, t).start()

        @pl.when(t > 0)
        def _():
            downward(k, t).start()

    def u_copy(k, sender, target):
        return pltpu.make_async_remote_copy(
            u_sum.at[k], u_all.at[k, sender], u_send.at[k, target], u_recv.at[k, sender],
            device_id={"tensor": target}, device_id_type=MESH)

    def h_copy(sender, target):
        return pltpu.make_async_remote_copy(
            h_sum, h_all.at[sender], h_send.at[target], h_recv.at[sender],
            device_id={"tensor": target}, device_id_type=MESH)

    def pool_copy(source, dest, send, recv):
        return pltpu.make_async_remote_copy(
            source, dest, send, recv, device_id={"pool": q}, device_id_type=MESH)

    def section_copy(k):
        return pltpu.make_async_remote_copy(
            grad_in.at[rows(k)], gath.at[t, rows(k)], s_send.at[k], s_recv.at[k],
            device_id={"section": jnp.maximum(s - 1, 0)}, device_id_type=MESH)

    def others(body):
        def run(i, _):
            body(lax.rem(t + i, n))
            return 0

        lax.fori_loop(1, n, run, 0)

    @pl.when(s == top)
    def _():
        gath[t] = cot[...]

        def first(k, _):
            own_start(k)
            return 0

        lax.fori_loop(0, min(AHEAD, tiles), first, 0)

    mine = pl.ds(pl.multiple_of(p * width, width), width)
    theirs = pl.ds(pl.multiple_of(q * width, width), width)
    seg_slot = [slot_of[seg_adapter[j]] for j in range(segs)]
    for j in range(segs):
        local = jnp.clip(seg_slot[j] - p * slots, 0, slots - 1)
        put_b[j] = panel_b[local, :, theirs]
        sel_b[0, j] = panel_b[local, :, mine]
    copy_b = pool_copy(put_b, sel_b.at[1], sel_send.at[0], sel_recv.at[0])
    copy_b.start()
    for j in range(segs):
        local = jnp.clip(seg_slot[j] - p * slots, 0, slots - 1)
        put_a[j] = panel_a[local, :, theirs]
        sel_a[0, j] = panel_a[local, :, mine]
    copy_a = pool_copy(put_a, sel_a.at[1], sel_send.at[1], sel_recv.at[1])
    copy_a.start()
    copy_b.wait()
    copy_a.wait()

    def chosen(k, sel):
        total, segment = jnp.int32(0), jnp.int32(0)
        for j in range(segs - 1):
            total = total + seg_tiles[j]
            segment = segment + (total <= k).astype(jnp.int32)
        slot = slot_of[seg_adapter[segment]]
        home = (slot >= p * slots) & (slot < (p + 1) * slots)
        return sel[1 - home.astype(jnp.int32), segment]

    def launch(k):
        @pl.when(s < top)
        def _():
            section_copy(k).wait_recv()
            own_start(k)

        u_part[k] = row_dot(chosen(k, sel_b), gath[t, rows(k)])
        pool_copy(u_part.at[k], u_pool.at[k], up_send.at[k], up_recv.at[k]).start()

    def shrink_x(k, _):
        h_part[:, rows(k)] = row_dot(chosen(k, sel_a), x[rows(k)])
        return 0

    lax.fori_loop(0, tiles, shrink_x, 0)
    h_pool_copy = pool_copy(h_part, h_pool, hp_send, hp_recv)
    h_pool_copy.start()
    h_pool_copy.wait()
    h_sum[...] = (h_part[...] + h_pool[...]).astype(BF16)

    @pl.when(s < top)
    def _():
        others(lambda tt: h_copy(t, tt).start())

    w_copy.wait()
    launch(0)

    def multiply(k, tt, half, acc, fresh):
        def one(b, _):
            r = pl.multiple_of(b * block, block)
            wr = pl.ds(pl.multiple_of(half * width + r, block), block)
            wc = pl.ds(pl.multiple_of(tt * width, width), width)
            product = row_dot(gath[tt, rows(k)], w[wr, wc])
            if fresh:
                acc[:, pl.ds(r, block)] = product
            else:
                acc[:, pl.ds(r, block)] += product
            return 0

        lax.fori_loop(0, width // block, one, 0)

    def arrive(k, d):
        low, high = jnp.maximum(t - d, 0), jnp.minimum(t + d, n - 1)

        @pl.when(t - d >= 0)
        def _():
            block_copy(k, low, low, g_send.at[k, low]).wait_recv()

            @pl.when(t < n - 1)
            def _():
                upward(k, low).start()

        @pl.when(t + d < n)
        def _():
            block_copy(k, high, high, g_send.at[k, high]).wait_recv()

            @pl.when(t > 0)
            def _():
                downward(k, high).start()

    def both(k, d, half, acc):
        @pl.when(t - d >= 0)
        def _():
            multiply(k, jnp.maximum(t - d, 0), half, acc, False)

        @pl.when(t + d < n)
        def _():
            multiply(k, jnp.minimum(t + d, n - 1), half, acc, False)

    def process(k, _):
        pool_copy(u_part.at[k], u_pool.at[k], up_send.at[k], up_recv.at[k]).wait()
        u_sum[k] = (u_part[k] + u_pool[k]).astype(BF16)
        others(lambda tt: u_copy(k, t, tt).start())

        send = part.at[k]
        multiply(k, t, q, send, True)
        multiply(k, t, p, own_acc, True)

        def middle(d, _):
            arrive(k, d)
            both(k, d, q, send)
            both(k, d, p, own_acc)
            return 0

        lax.fori_loop(1, n - 1, middle, 0)

        @pl.when((s == top) & (k + AHEAD < tiles))
        def _():
            own_start(k + AHEAD)

        @pl.when(k + 1 < tiles)
        def _():
            launch(k + 1)

        arrive(k, n - 1)
        both(k, n - 1, q, send)
        half_copy = pool_copy(send, part_in.at[k], pp_send.at[k], pp_recv.at[k])
        half_copy.start()
        both(k, n - 1, p, own_acc)
        u_all[k, t] = u_sum[k]
        others(lambda tt: u_copy(k, tt, tt).wait_recv())
        u = u_all[k, 0].astype(F32)
        for i in range(1, n):
            u = u + u_all[k, i].astype(F32)
        low_u[:, rows(k)] = u.astype(BF16)
        expand = jnp.dot(u.T.astype(BF16), chosen(k, sel_a), preferred_element_type=F32)
        half_copy.wait()
        grad_in[rows(k)] = (own_acc[...] + part_in[k] + SCALE * expand).astype(BF16)

        @pl.when(s > 0)
        def _():
            section_copy(k).start()

        return 0

    lax.fori_loop(0, tiles, process, 0)

    @pl.when(s == top)
    def _():
        others(lambda tt: h_copy(t, tt).start())

    grad_own[...] = gath[t]
    h_all[t] = h_sum[...]
    others(lambda tt: h_copy(tt, tt).wait_recv())
    h = h_all[0].astype(F32)
    for i in range(1, n):
        h = h + h_all[i].astype(F32)
    low_h[...] = h.astype(BF16)

    def sent(tt):
        h_copy(t, tt).wait_send()

        def one(k, _):
            u_copy(k, t, tt).wait_send()

            @pl.when((tt < t) & (t < n - 1))
            def _():
                upward(k, tt).wait_send()

            @pl.when((tt > t) & (t > 0))
            def _():
                downward(k, tt).wait_send()

            return 0

        lax.fori_loop(0, tiles, one, 0)

    others(sent)

    def own_sent(k, _):
        @pl.when(t < n - 1)
        def _():
            upward(k, t).wait_send()

        @pl.when(t > 0)
        def _():
            downward(k, t).wait_send()

        return 0

    lax.fori_loop(0, tiles, own_sent, 0)

    @pl.when(s > 0)
    def _():
        def one(k, _):
            section_copy(k).wait_send()
            return 0

        lax.fori_loop(0, tiles, one, 0)


def per_device(cotangent, saved_inputs, base_weight, panel_a, panel_b, seg_tiles, seg_adapter, slot_of):
    n = lax.axis_size("tensor")
    micro, row_count, width = cotangent.shape
    m = micro * row_count
    tiles = m // TILE
    weight = base_weight[0].reshape(base_weight.shape[1], -1)
    x = saved_inputs[0].reshape(m, width)
    rank = panel_a.shape[2]
    segs = seg_tiles.shape[0]
    smem = pl.BlockSpec(memory_space=pltpu.SMEM)
    vmem = pl.BlockSpec(memory_space=pltpu.VMEM)
    dma = pltpu.SemaphoreType.DMA
    grad_in, grad_own, low_u, low_h = pl.pallas_call(
        kernel,
        out_shape=(
            jax.ShapeDtypeStruct((m, width), BF16),
            jax.ShapeDtypeStruct((m, width), BF16),
            jax.ShapeDtypeStruct((rank, m), BF16),
            jax.ShapeDtypeStruct((rank, m), BF16),
        ),
        in_specs=[smem] * 3 + [vmem] * 2 + [pl.BlockSpec(memory_space=pl.ANY)] + [vmem] * 2,
        out_specs=(vmem,) * 4,
        scratch_shapes=[
            pltpu.VMEM(weight.shape, BF16),
            pltpu.VMEM((n, m, width), BF16),
            pltpu.VMEM((tiles, TILE, width), F32),
            pltpu.VMEM((tiles, TILE, width), F32),
            pltpu.VMEM((TILE, width), F32),
            pltpu.VMEM((2, segs, rank, width), BF16),
            pltpu.VMEM((2, segs, rank, width), BF16),
            pltpu.VMEM((segs, rank, width), BF16),
            pltpu.VMEM((segs, rank, width), BF16),
            pltpu.VMEM((tiles, rank, TILE), F32),
            pltpu.VMEM((tiles, rank, TILE), F32),
            pltpu.VMEM((tiles, rank, TILE), BF16),
            pltpu.VMEM((tiles, n, rank, TILE), BF16),
            pltpu.VMEM((rank, m), F32),
            pltpu.VMEM((rank, m), F32),
            pltpu.VMEM((rank, m), BF16),
            pltpu.VMEM((n, rank, m), BF16),
            dma(()),
            dma((tiles, n)), dma((tiles,)), dma((tiles, n)), dma((tiles, n)), dma((tiles, n)),
            dma((tiles,)), dma((tiles,)), dma((tiles,)), dma((tiles,)),
            dma((2,)), dma((2,)), dma(()), dma(()), dma((n,)), dma((n,)),
            dma((tiles,)), dma((tiles,)),
        ],
        compiler_params=pltpu.CompilerParams(
            collective_id=0, has_side_effects=True, vmem_limit_bytes=58 * 1024 * 1024),
    )(seg_tiles, seg_adapter, slot_of, cotangent.reshape(m, width), x, weight, panel_a[0], panel_b[0])

    adapters = slot_of.shape[0]
    owners = jnp.repeat(tile_owners(seg_tiles, seg_adapter, tiles), TILE)
    hit = owners[None, :] == jnp.arange(adapters, dtype=jnp.int32)[:, None]

    def spread(low, wide):
        lanes = jnp.where(hit[:, None, :], low[None], jnp.zeros((), BF16)).reshape(adapters * rank, m)
        full = SCALE * jnp.dot(lanes, wide, preferred_element_type=F32)
        return full.reshape(1, adapters, rank, width)

    return (grad_in.reshape(1, micro, row_count, width), spread(low_u, x), spread(low_h, grad_own))


def solution(mesh):
    placed = (
        P("groups", None, ("tensor", "pool")),
        P("section", "groups", None, ("tensor", "pool")),
        P("section", "tensor", None, "pool", None),
        P("section", "pool", None, "tensor"),
        P("section", "pool", None, "tensor"),
        P("groups"),
        P("groups"),
        P(),
    )
    out = P("section", "groups", None, ("tensor", "pool"))
    return jax.shard_map(
        per_device, mesh=mesh, in_specs=placed, out_specs=(out, out, out), check_vma=False)
```

```python
import jax
import jax.numpy as jnp
from jax import lax
from jax.experimental import pallas as pl
from jax.experimental.pallas import tpu as pltpu
from jax.sharding import PartitionSpec as P

TILE = 128
SCALE = 0.5
AHEAD = 2
MESH = pl.DeviceIdType.MESH
F32 = jnp.float32
BF16 = jnp.bfloat16


def tile_owners(seg_tiles, seg_adapter, tiles):
    segs = seg_tiles.shape[0]
    ends = jnp.cumsum(seg_tiles)
    places = jnp.arange(tiles, dtype=jnp.int32)
    segment = jnp.sum((ends[None, :] <= places[:, None]).astype(jnp.int32), axis=1)
    picks = segment[:, None] == jnp.arange(segs, dtype=jnp.int32)[None, :]
    return jnp.sum(jnp.where(picks, seg_adapter[None, :], 0), axis=1)


def row_dot(a, b):
    return lax.dot_general(a, b, (((1,), (1,)), ((), ())), preferred_element_type=F32)


def kernel(
    seg_tiles, seg_adapter, slot_of, cot, x, w_hbm, panel_a, panel_b,
    grad_in, grad_own, low_u, low_h,
    w, w_raw, gath, part, part_in, own_acc, sel_a, sel_b, put_a, put_b,
    u_part, u_pool, u_sum, u_all, h_part, h_pool, h_sum, h_all,
    w_sem, g_send, g_down, g_recv, u_send, u_recv, up_send, up_recv, pp_send, pp_recv,
    sel_send, sel_recv, hp_send, hp_recv, h_send, h_recv, s_send, s_recv,
):
    n = lax.axis_size("tensor")
    top = lax.axis_size("section") - 1
    s, t, p = lax.axis_index("section"), lax.axis_index("tensor"), lax.axis_index("pool")
    q = 1 - p
    rows_all, width = cot.shape
    tiles = rows_all // TILE
    segs = seg_tiles.shape[0]
    slots = panel_a.shape[0]
    block = min(256, width)

    barrier = pltpu.get_barrier_semaphore()

    def greet(i, _):
        pl.semaphore_signal(barrier, inc=1, device_id={"tensor": lax.rem(t + i, n)}, device_id_type=MESH)
        return 0

    lax.fori_loop(1, n, greet, 0)
    pl.semaphore_signal(barrier, inc=1, device_id={"pool": q}, device_id_type=MESH)

    @pl.when(s > 0)
    def _():
        pl.semaphore_signal(barrier, inc=1, device_id={"section": s - 1}, device_id_type=MESH)

    @pl.when(s < top)
    def _():
        pl.semaphore_signal(barrier, inc=1, device_id={"section": s + 1}, device_id_type=MESH)

    parts = w_hbm.shape[0] // block

    def w_copy(b):
        slot = lax.rem(b, 2)
        source = w_hbm.at[pl.ds(pl.multiple_of(b * block, block), block)]
        return pltpu.make_async_copy(source, w_raw.at[slot], w_sem.at[slot])

    w_copy(jnp.int32(0)).start()
    pl.semaphore_wait(barrier, n + (s > 0).astype(jnp.int32) + (s < top).astype(jnp.int32))

    def rows(k):
        return pl.ds(pl.multiple_of(k * TILE, TILE), TILE)

    def block_copy(k, owner, target, sem):
        place = gath.at[owner, rows(k)]
        return pltpu.make_async_remote_copy(
            place, place, sem, g_recv.at[k, owner],
            device_id={"tensor": target}, device_id_type=MESH)

    def upward(k, owner):
        return block_copy(k, owner, jnp.minimum(t + 1, n - 1), g_send.at[k, owner])

    def downward(k, owner):
        sem = g_send.at[k, owner] if owner is not t else g_down.at[k]
        return block_copy(k, owner, jnp.maximum(t - 1, 0), sem)

    def own_start(k):
        @pl.when(t < n - 1)
        def _():
            upward(k, t).start()

        @pl.when(t > 0)
        def _():
            downward(k, t).start()

    def u_copy(k, sender, target):
        return pltpu.make_async_remote_copy(
            u_sum.at[k], u_all.at[k, sender], u_send.at[k, target], u_recv.at[k, sender],
            device_id={"tensor": target}, device_id_type=MESH)

    def h_copy(sender, target):
        return pltpu.make_async_remote_copy(
            h_sum, h_all.at[sender], h_send.at[target], h_recv.at[sender],
            device_id={"tensor": target}, device_id_type=MESH)

    def pool_copy(source, dest, send, recv):
        return pltpu.make_async_remote_copy(
            source, dest, send, recv, device_id={"pool": q}, device_id_type=MESH)

    def section_copy(k):
        return pltpu.make_async_remote_copy(
            grad_in.at[rows(k)], gath.at[t, rows(k)], s_send.at[k], s_recv.at[k],
            device_id={"section": jnp.maximum(s - 1, 0)}, device_id_type=MESH)

    def others(body):
        def run(i, _):
            body(lax.rem(t + i, n))
            return 0

        lax.fori_loop(1, n, run, 0)

    @pl.when(s == top)
    def _():
        gath[t] = cot[...]

        def first(k, _):
            own_start(k)
            return 0

        lax.fori_loop(0, min(AHEAD, tiles), first, 0)

    mine = pl.ds(pl.multiple_of(p * width, width), width)
    theirs = pl.ds(pl.multiple_of(q * width, width), width)
    seg_slot = [slot_of[seg_adapter[j]] for j in range(segs)]
    for j in range(segs):
        local = jnp.clip(seg_slot[j] - p * slots, 0, slots - 1)
        put_b[j] = panel_b[local, :, theirs]
        sel_b[0, j] = panel_b[local, :, mine]
    copy_b = pool_copy(put_b, sel_b.at[1], sel_send.at[0], sel_recv.at[0])
    copy_b.start()
    for j in range(segs):
        local = jnp.clip(seg_slot[j] - p * slots, 0, slots - 1)
        put_a[j] = panel_a[local, :, theirs]
        sel_a[0, j] = panel_a[local, :, mine]
    copy_a = pool_copy(put_a, sel_a.at[1], sel_send.at[1], sel_recv.at[1])
    copy_a.start()
    copy_b.wait()
    copy_a.wait()

    def chosen(k, sel):
        total, segment = jnp.int32(0), jnp.int32(0)
        for j in range(segs - 1):
            total = total + seg_tiles[j]
            segment = segment + (total <= k).astype(jnp.int32)
        slot = slot_of[seg_adapter[segment]]
        home = (slot >= p * slots) & (slot < (p + 1) * slots)
        return sel[1 - home.astype(jnp.int32), segment]

    def launch(k):
        @pl.when(s < top)
        def _():
            section_copy(k).wait_recv()
            own_start(k)

        u_part[k] = row_dot(chosen(k, sel_b), gath[t, rows(k)])
        pool_copy(u_part.at[k], u_pool.at[k], up_send.at[k], up_recv.at[k]).start()

    def shrink_x(k, _):
        h_part[:, rows(k)] = row_dot(chosen(k, sel_a), x[rows(k)])
        return 0

    lax.fori_loop(0, tiles, shrink_x, 0)
    h_pool_copy = pool_copy(h_part, h_pool, hp_send, hp_recv)
    h_pool_copy.start()
    h_pool_copy.wait()
    h_sum[...] = (h_part[...] + h_pool[...]).astype(BF16)

    @pl.when(s < top)
    def _():
        others(lambda tt: h_copy(t, tt).start())

    def unpack(b, _):
        @pl.when(b + 1 < parts)
        def _():
            w_copy(b + 1).start()

        w_copy(b).wait()
        raw = w_raw.at[lax.rem(b, 2)]
        step = min(64, block)

        def rows_of(i, _):
            r = pl.multiple_of(i * step, step)
            piece = raw[pl.ds(r, step)].astype(F32)
            for tt in range(n):
                w[pl.ds(pl.multiple_of(b * block + r, step), step), tt * width:(tt + 1) * width] = piece[:, tt].astype(BF16)
            return 0

        lax.fori_loop(0, block // step, rows_of, 0)
        return 0

    lax.fori_loop(0, parts, unpack, 0)
    launch(0)

    def multiply(k, tt, half, acc, fresh):
        def one(b, _):
            r = pl.multiple_of(b * block, block)
            wr = pl.ds(pl.multiple_of(half * width + r, block), block)
            wc = pl.ds(pl.multiple_of(tt * width, width), width)
            product = row_dot(gath[tt, rows(k)], w[wr, wc])
            if fresh:
                acc[:, pl.ds(r, block)] = product
            else:
                acc[:, pl.ds(r, block)] += product
            return 0

        lax.fori_loop(0, width // block, one, 0)

    def arrive(k, d):
        low, high = jnp.maximum(t - d, 0), jnp.minimum(t + d, n - 1)

        @pl.when(t - d >= 0)
        def _():
            block_copy(k, low, low, g_send.at[k, low]).wait_recv()

            @pl.when(t < n - 1)
            def _():
                upward(k, low).start()

        @pl.when(t + d < n)
        def _():
            block_copy(k, high, high, g_send.at[k, high]).wait_recv()

            @pl.when(t > 0)
            def _():
                downward(k, high).start()

    def both(k, d, half, acc):
        @pl.when(t - d >= 0)
        def _():
            multiply(k, jnp.maximum(t - d, 0), half, acc, False)

        @pl.when(t + d < n)
        def _():
            multiply(k, jnp.minimum(t + d, n - 1), half, acc, False)

    def process(k, _):
        pool_copy(u_part.at[k], u_pool.at[k], up_send.at[k], up_recv.at[k]).wait()
        u_sum[k] = (u_part[k] + u_pool[k]).astype(BF16)
        others(lambda tt: u_copy(k, t, tt).start())

        send = part.at[k]
        multiply(k, t, q, send, True)
        multiply(k, t, p, own_acc, True)

        def middle(d, _):
            arrive(k, d)
            both(k, d, q, send)
            both(k, d, p, own_acc)
            return 0

        lax.fori_loop(1, n - 1, middle, 0)

        @pl.when((s == top) & (k + AHEAD < tiles))
        def _():
            own_start(k + AHEAD)

        @pl.when(k + 1 < tiles)
        def _():
            launch(k + 1)

        arrive(k, n - 1)
        both(k, n - 1, q, send)
        half_copy = pool_copy(send, part_in.at[k], pp_send.at[k], pp_recv.at[k])
        half_copy.start()
        both(k, n - 1, p, own_acc)
        u_all[k, t] = u_sum[k]
        others(lambda tt: u_copy(k, tt, tt).wait_recv())
        u = u_all[k, 0].astype(F32)
        for i in range(1, n):
            u = u + u_all[k, i].astype(F32)
        low_u[:, rows(k)] = u.astype(BF16)
        expand = jnp.dot(u.T.astype(BF16), chosen(k, sel_a), preferred_element_type=F32)
        half_copy.wait()
        grad_in[rows(k)] = (own_acc[...] + part_in[k] + SCALE * expand).astype(BF16)

        @pl.when(s > 0)
        def _():
            section_copy(k).start()

        return 0

    lax.fori_loop(0, tiles, process, 0)

    @pl.when(s == top)
    def _():
        others(lambda tt: h_copy(t, tt).start())

    grad_own[...] = gath[t]
    h_all[t] = h_sum[...]
    others(lambda tt: h_copy(tt, tt).wait_recv())
    h = h_all[0].astype(F32)
    for i in range(1, n):
        h = h + h_all[i].astype(F32)
    low_h[...] = h.astype(BF16)

    def sent(tt):
        h_copy(t, tt).wait_send()

        def one(k, _):
            u_copy(k, t, tt).wait_send()

            @pl.when((tt < t) & (t < n - 1))
            def _():
                upward(k, tt).wait_send()

            @pl.when((tt > t) & (t > 0))
            def _():
                downward(k, tt).wait_send()

            return 0

        lax.fori_loop(0, tiles, one, 0)

    others(sent)

    def own_sent(k, _):
        @pl.when(t < n - 1)
        def _():
            upward(k, t).wait_send()

        @pl.when(t > 0)
        def _():
            downward(k, t).wait_send()

        return 0

    lax.fori_loop(0, tiles, own_sent, 0)

    @pl.when(s > 0)
    def _():
        def one(k, _):
            section_copy(k).wait_send()
            return 0

        lax.fori_loop(0, tiles, one, 0)


def per_device(cotangent, saved_inputs, base_weight, panel_a, panel_b, seg_tiles, seg_adapter, slot_of):
    n = lax.axis_size("tensor")
    micro, row_count, width = cotangent.shape
    m = micro * row_count
    tiles = m // TILE
    weight = base_weight[0].reshape(base_weight.shape[1], n, width)
    x = saved_inputs[0].reshape(m, width)
    rank = panel_a.shape[2]
    segs = seg_tiles.shape[0]
    smem = pl.BlockSpec(memory_space=pltpu.SMEM)
    vmem = pl.BlockSpec(memory_space=pltpu.VMEM)
    dma = pltpu.SemaphoreType.DMA
    grad_in, grad_own, low_u, low_h = pl.pallas_call(
        kernel,
        out_shape=(
            jax.ShapeDtypeStruct((m, width), BF16),
            jax.ShapeDtypeStruct((m, width), BF16),
            jax.ShapeDtypeStruct((rank, m), BF16),
            jax.ShapeDtypeStruct((rank, m), BF16),
        ),
        in_specs=[smem] * 3 + [vmem] * 2 + [pl.BlockSpec(memory_space=pl.ANY)] + [vmem] * 2,
        out_specs=(vmem,) * 4,
        scratch_shapes=[
            pltpu.VMEM((weight.shape[0], n * width), BF16),
            pltpu.VMEM((2, min(256, width), n, width), BF16),
            pltpu.VMEM((n, m, width), BF16),
            pltpu.VMEM((tiles, TILE, width), F32),
            pltpu.VMEM((tiles, TILE, width), F32),
            pltpu.VMEM((TILE, width), F32),
            pltpu.VMEM((2, segs, rank, width), BF16),
            pltpu.VMEM((2, segs, rank, width), BF16),
            pltpu.VMEM((segs, rank, width), BF16),
            pltpu.VMEM((segs, rank, width), BF16),
            pltpu.VMEM((tiles, rank, TILE), F32),
            pltpu.VMEM((tiles, rank, TILE), F32),
            pltpu.VMEM((tiles, rank, TILE), BF16),
            pltpu.VMEM((tiles, n, rank, TILE), BF16),
            pltpu.VMEM((rank, m), F32),
            pltpu.VMEM((rank, m), F32),
            pltpu.VMEM((rank, m), BF16),
            pltpu.VMEM((n, rank, m), BF16),
            dma((2,)),
            dma((tiles, n)), dma((tiles,)), dma((tiles, n)), dma((tiles, n)), dma((tiles, n)),
            dma((tiles,)), dma((tiles,)), dma((tiles,)), dma((tiles,)),
            dma((2,)), dma((2,)), dma(()), dma(()), dma((n,)), dma((n,)),
            dma((tiles,)), dma((tiles,)),
        ],
        compiler_params=pltpu.CompilerParams(
            collective_id=0, has_side_effects=True, vmem_limit_bytes=58 * 1024 * 1024),
    )(seg_tiles, seg_adapter, slot_of, cotangent.reshape(m, width), x, weight, panel_a[0], panel_b[0])

    adapters = slot_of.shape[0]
    owners = jnp.repeat(tile_owners(seg_tiles, seg_adapter, tiles), TILE)
    hit = owners[None, :] == jnp.arange(adapters, dtype=jnp.int32)[:, None]

    def spread(low, wide):
        lanes = jnp.where(hit[:, None, :], low[None], jnp.zeros((), BF16)).reshape(adapters * rank, m)
        full = SCALE * jnp.dot(lanes, wide, preferred_element_type=F32)
        return full.reshape(1, adapters, rank, width)

    return (grad_in.reshape(1, micro, row_count, width), spread(low_u, x), spread(low_h, grad_own))


def solution(mesh):
    placed = (
        P("groups", None, ("tensor", "pool")),
        P("section", "groups", None, ("tensor", "pool")),
        P("section", "tensor", None, "pool", None),
        P("section", "pool", None, "tensor"),
        P("section", "pool", None, "tensor"),
        P("groups"),
        P("groups"),
        P(),
    )
    out = P("section", "groups", None, ("tensor", "pool"))
    return jax.shard_map(
        per_device, mesh=mesh, in_specs=placed, out_specs=(out, out, out), check_vma=False)
```
